32 devices in a mesh: wide: 8 (over z, x), narrow: 4 (over y, core).
Axes of the slice: x: 2, y: 2, z: 4, core: 2. Of those that a mesh axis runs over, the one named last changes fastest.
Arguments:
- activations: bfloat16 [64, 8192], P('wide', 'narrow'), may hold values from -6 to 6
- up_weight: bfloat16 [8192, 28672], P('narrow', 'wide'), may hold values from -0.0625 to 0.0625
- block_mask: int32 [128, 448], P('narrow', 'wide'), may hold values from 0 to 1, as said below
- out_grad: bfloat16 [64, 28672], P('narrow', 'wide'), may hold values from -6 to 6
Outputs:
- output: bfloat16 [64, 28672], P('narrow', 'wide')
- input_grad: bfloat16 [64, 8192], P('wide', 'narrow')
- weight_grad: bfloat16 [8192, 28672], P('narrow', 'wide')
The draws below stay inside these ranges and needn't reach their ends.
Inputs may be any that keep to these rules, and one draw needn't show every extreme that they name: block_mask holds 0 or 1; the share of kept blocks differs from one block column to another.
All inputs are finite; a program needn't handle non-finite values.
Results may differ from the reference program's by a relative error of at most 0.012.
Values may be sent and summed in bfloat16 or wider, within the bound.
A program may use at most 192 MiB of HBM per device.

```python
import jax
import jax.numpy as jnp
from jax import lax

D = 8192
FF = 28672
BLOCK = 64
TOKENS = 64
DB = 128
FB = 448


def draw_block_mask(key, part):
    first_key, second_key = jax.random.split(jax.random.fold_in(key, 11))
    keep_share = jax.random.randint(first_key, (1, FB), 10, 91)
    rolled = jax.random.randint(second_key, (DB, FB), 0, 100)
    return (rolled < keep_share).astype(jnp.int32)


def block_levels(key, dims, cuts, least, high):
    def one(axis_at, shards_of):
        heights = jax.random.uniform(jax.random.fold_in(jax.random.fold_in(key, 6), axis_at), (shards_of,), jnp.float32, least / len(cuts), high / len(cuts))
        return jnp.repeat(jnp.exp(heights), dims[axis_at] // shards_of).reshape((-1,) + (1,) * (len(dims) - axis_at - 1))

    gain = one(*cuts[0])
    for cut in cuts[1:]:
        gain = gain * one(*cut)
    return gain


def normal_values(key, shape, width, reach, shards=(), kind=jnp.bfloat16):
    result = width * jax.random.normal(key, shape, jnp.float32)
    if shards:
        result = result * block_levels(key, shape, shards, -0.22, 0.18)
    return jnp.clip(result, -reach, reach).astype(kind)


def setup_inputs(seed: int = 0) -> dict:
    key_of = jax.random.split(jax.random.key(seed), 5)
    activations = normal_values(key_of[0], (TOKENS, D), 1.0, 6.0, ((0, 8), (1, 4)))
    up_weight = normal_values(key_of[1], (D, FF), D ** -0.5, 0.0625, ((0, 4), (1, 8)))
    block_mask = draw_block_mask(jax.random.fold_in(key_of[4], 71), 0)
    out_grad = normal_values(key_of[3], (TOKENS, FF), 1.0, 6.0, ((0, 4), (1, 8)))
    return {"activations": activations, "up_weight": up_weight, "block_mask": block_mask, "out_grad": out_grad}


def apply_mask(weight, blocks):
    rows_b, cols_b = blocks.shape
    shaped = weight.reshape(rows_b, BLOCK, cols_b, BLOCK)
    return (shaped * blocks[:, None, :, None].astype(weight.dtype)).reshape(weight.shape)


def reference(activations, up_weight, block_mask, out_grad):
    masked = apply_mask(up_weight, block_mask)
    output = jnp.dot(activations, masked, preferred_element_type=jnp.float32).astype(jnp.bfloat16)
    input_grad = lax.dot_general(out_grad, masked, (((1,), (1,)), ((), ())), preferred_element_type=jnp.float32).astype(jnp.bfloat16)
    full_grad = lax.dot_general(activations, out_grad, (((0,), (0,)), ((), ())), preferred_element_type=jnp.float32)
    weight_grad = apply_mask(full_grad, block_mask).astype(jnp.bfloat16)
    return (output, input_grad, weight_grad)
```

```python
import functools

import jax
import jax.numpy as jnp
from jax import lax
from jax.experimental import pallas as pl
from jax.experimental.pallas import tpu as pltpu
from jax.sharding import PartitionSpec as P

MESH = pl.DeviceIdType.MESH
BF16 = jnp.bfloat16
F32 = jnp.float32
ROWS = 256


def column_chunk(cols):
    return 512 if cols % 512 == 0 else cols


def exchange_kernel(
    nw, nn, side,
    act_ref, w_hbm, mask_ref, og_ref,
    out_ref, ig_ref, act_out, og_out, mask_out,
    w, act_all, og_all, ig_part, ig_recv, out_part, out_recv,
    w_sem, act_send, act_recv, og_send, og_recv, ig_send, ig_rsem, out_send, out_rsem,
):
    iw = lax.axis_index("wide")
    jn = lax.axis_index("narrow")
    rows, cols = w_hbm.shape
    steps = rows // ROWS
    blocks = ROWS // side
    tokens = nw * act_ref.shape[0]

    def fetch(c):
        at = pl.ds(pl.multiple_of(c * ROWS, ROWS), ROWS)
        return pltpu.make_async_copy(w_hbm.at[at], w.at[at], w_sem.at[c])

    for c in range(steps):
        fetch(c).start()

    barrier = pltpu.get_barrier_semaphore()
    for off in range(1, nw):
        pl.semaphore_signal(
            barrier, inc=1, device_id={"wide": lax.rem(iw + off, nw)}, device_id_type=MESH
        )
    for off in range(1, nn):
        pl.semaphore_signal(
            barrier, inc=1, device_id={"narrow": lax.rem(jn + off, nn)}, device_id_type=MESH
        )

    at_col = lax.broadcasted_iota(jnp.int32, (cols // side, cols), 1)
    at_row = lax.broadcasted_iota(jnp.int32, (cols // side, cols), 0)
    low = at_row * side
    spread = jnp.where((at_col >= low) & (at_col < low + side), 1.0, 0.0).astype(BF16)
    mask_out[...] = jnp.dot(
        mask_ref[...].astype(F32).astype(BF16), spread, preferred_element_type=F32
    )
    act_all[iw] = act_ref[...]
    og_all[jn] = og_ref[...]

    pl.semaphore_wait(barrier, nw + nn - 2)

    def wide_copy(src, dst, send, recv, off):
        return pltpu.make_async_remote_copy(
            src_ref=src, dst_ref=dst, send_sem=send.at[off], recv_sem=recv.at[off],
            device_id={"wide": lax.rem(iw + off, nw)}, device_id_type=MESH,
        )

    def narrow_copy(src, dst, send, recv, off):
        return pltpu.make_async_remote_copy(
            src_ref=src, dst_ref=dst, send_sem=send.at[off], recv_sem=recv.at[off],
            device_id={"narrow": lax.rem(jn + off, nn)}, device_id_type=MESH,
        )

    og_copies = [
        narrow_copy(og_ref, og_all.at[jn], og_send, og_recv, off) for off in range(1, nn)
    ]
    act_copies = [
        wide_copy(act_ref, act_all.at[iw], act_send, act_recv, off) for off in range(1, nw)
    ]
    for copy in og_copies + act_copies:
        copy.start()

    @pl.loop(0, steps)
    def _(c):
        fetch(c).wait()
        for b in range(blocks):
            kept = mask_out[pl.ds(c * blocks + b, 1), :].astype(BF16)
            at = pl.ds(pl.multiple_of(c * ROWS + b * side, side), side)
            w[at, :] = w[at, :] * kept

    for copy in og_copies:
        copy.wait()
    og_out[...] = og_all[...].reshape(tokens, cols)

    @pl.loop(0, steps)
    def _(c):
        at = pl.ds(pl.multiple_of(c * ROWS, ROWS), ROWS)
        part = lax.dot_general(
            og_out[...], w[at, :], (((1,), (1,)), ((), ())), preferred_element_type=F32
        )
        ig_part[:, :, at] = part.reshape(nw, tokens // nw, ROWS).astype(BF16)

    ig_copies = [
        wide_copy(
            ig_part.at[lax.rem(iw + off, nw)], ig_recv.at[off], ig_send, ig_rsem, off
        )
        for off in range(1, nw)
    ]
    for copy in ig_copies:
        copy.start()

    for copy in act_copies:
        copy.wait()
    act_out[...] = act_all[...].astype(F32).reshape(tokens, rows).astype(BF16)

    wide_cols = column_chunk(cols)

    @pl.loop(0, cols // wide_cols)
    def _(c):
        at = pl.ds(pl.multiple_of(c * wide_cols, 128) if wide_cols < cols else 0, wide_cols)
        part = jnp.dot(act_out[...], w[:, at], preferred_element_type=F32)
        out_part[:, :, at] = part.astype(BF16).reshape(nn, tokens // nn, wide_cols)

    out_copies = [
        narrow_copy(
            out_part.at[lax.rem(jn + off, nn)], out_recv.at[off], out_send, out_rsem, off
        )
        for off in range(1, nn)
    ]
    for copy in out_copies:
        copy.start()

    for copy in ig_copies:
        copy.wait()
    total = ig_part[iw].astype(F32)
    for off in range(1, nw):
        total = total + ig_recv[off].astype(F32)
    ig_ref[...] = total.astype(BF16)

    for copy in out_copies:
        copy.wait()
    total = out_part[jn].astype(F32)
    for off in range(1, nn):
        total = total + out_recv[off].astype(F32)
    out_ref[...] = total.astype(BF16)


def weight_kernel(side, act_ref, og_ref, mask_ref, grad_ref):
    step = pl.program_id(0)
    high, cols = grad_ref.shape
    blocks = high // side
    chunk = column_chunk(cols)
    turned = act_ref[...].T

    for c in range(cols // chunk):
        at = slice(c * chunk, (c + 1) * chunk)
        grad = jnp.dot(turned, og_ref[:, at], preferred_element_type=F32).astype(BF16)
        for b in range(blocks):
            kept = mask_ref[pl.ds(step * blocks + b, 1), at].astype(BF16)
            grad_ref[b * side:(b + 1) * side, at] = grad[b * side:(b + 1) * side] * kept


def on_device(nw, nn, activations, up_weight, block_mask, out_grad):
    rows, cols = up_weight.shape
    own_w, own_n = activations.shape[0], out_grad.shape[0]
    tokens = nw * own_w
    side = rows // block_mask.shape[0]
    vmem = pl.BlockSpec(memory_space=pltpu.VMEM)
    dma = pltpu.SemaphoreType.DMA
    output, input_grad, act_all, og_all, mask_wide = pl.pallas_call(
        functools.partial(exchange_kernel, nw, nn, side),
        out_shape=(
            jax.ShapeDtypeStruct((own_n, cols), BF16),
            jax.ShapeDtypeStruct((own_w, rows), BF16),
            jax.ShapeDtypeStruct((tokens, rows), BF16),
            jax.ShapeDtypeStruct((tokens, cols), BF16),
            jax.ShapeDtypeStruct((block_mask.shape[0], cols), F32),
        ),
        in_specs=[vmem, pl.BlockSpec(memory_space=pl.ANY), vmem, vmem],
        out_specs=(vmem,) * 5,
        scratch_shapes=[
            pltpu.VMEM((rows, cols), BF16),
            pltpu.VMEM((nw, own_w, rows), BF16),
            pltpu.VMEM((nn, own_n, cols), BF16),
            pltpu.VMEM((nw, own_w, rows), BF16),
            pltpu.VMEM((nw, own_w, rows), BF16),
            pltpu.VMEM((nn, own_n, cols), BF16),
            pltpu.VMEM((nn, own_n, cols), BF16),
            dma((rows // ROWS,)),
            dma((nw,)), dma((nw,)),
            dma((nn,)), dma((nn,)),
            dma((nw,)), dma((nw,)),
            dma((nn,)), dma((nn,)),
        ],
        compiler_params=pltpu.CompilerParams(
            collective_id=0, has_side_effects=True, vmem_limit_bytes=48 * 2**20
        ),
        cost_estimate=pl.CostEstimate(
            flops=4 * tokens * rows * cols, bytes_accessed=2 * rows * cols, transcendentals=0
        ),
        name="exchange",
    )(activations, up_weight, block_mask, out_grad)
    weight_grad = pl.pallas_call(
        functools.partial(weight_kernel, side),
        grid=(rows // ROWS,),
        out_shape=jax.ShapeDtypeStruct((rows, cols), BF16),
        in_specs=[
            pl.BlockSpec((tokens, ROWS), lambda i: (0, i)),
            pl.BlockSpec((tokens, cols), lambda i: (0, 0)),
            pl.BlockSpec(mask_wide.shape, lambda i: (0, 0)),
        ],
        out_specs=pl.BlockSpec((ROWS, cols), lambda i: (i, 0)),
        compiler_params=pltpu.CompilerParams(vmem_limit_bytes=32 * 2**20),
        cost_estimate=pl.CostEstimate(
            flops=2 * tokens * rows * cols, bytes_accessed=2 * rows * cols, transcendentals=0
        ),
        name="weight_grad",
    )(act_all, og_all, mask_wide)
    return (output, input_grad, weight_grad)


def solution(mesh):
    placed = (P("wide", "narrow"), P("narrow", "wide"), P("narrow", "wide"), P("narrow", "wide"))
    return jax.shard_map(
        functools.partial(on_device, mesh.shape["wide"], mesh.shape["narrow"]),
        mesh=mesh,
        in_specs=placed,
        out_specs=(P("narrow", "wide"), P("wide", "narrow"), P("narrow", "wide")),
        check_vma=False,
    )
```

```python
import functools

import jax
import jax.numpy as jnp
from jax import lax
from jax.experimental import pallas as pl
from jax.experimental.pallas import tpu as pltpu
from jax.sharding import PartitionSpec as P

MESH = pl.DeviceIdType.MESH
BF16 = jnp.bfloat16
F32 = jnp.float32
ROWS = 256


def column_chunk(cols):
    return 512 if cols % 512 == 0 else cols


def halves(count):
    middle = (count + 1) // 2
    return ((0, middle), (middle, count)) if count > 1 else ((0, count),)


def grad_rows(side, act_ref, og_ref, mask_ref, first, grad_ref, at):
    cols = og_ref.shape[1]
    tile_cols = 256 if cols % 256 == 0 else cols
    tile_rows = 2 * side
    turned = act_ref[:, pl.ds(first, ROWS)].T
    for r in range(ROWS // tile_rows):
        left = turned[r * tile_rows:(r + 1) * tile_rows]
        for c in range(cols // tile_cols):
            across = slice(c * tile_cols, (c + 1) * tile_cols)
            grad = jnp.dot(left, og_ref[:, across], preferred_element_type=F32).astype(BF16)
            for b in range(tile_rows // side):
                row = r * tile_rows + b * side
                kept = mask_ref[pl.ds((first + row) // side, 1), across].astype(BF16)
                grad_ref[pl.ds(at + row, side), across] = grad[b * side:(b + 1) * side] * kept


def exchange_kernel(
    nw, nn, side,
    act_hbm, w_hbm, mask_hbm, og_hbm,
    out_ref, ig_ref, act_out, og_out, mask_out, grad_out,
    w, mask, act_all, og_all, ig_part, ig_recv, out_part, out_recv,
    in_sem, w_sem, act_send, act_recv, og_send, og_recv,
    ig_send, ig_rsem, out_send, out_rsem,
):
    iw = lax.axis_index("wide")
    jn = lax.axis_index("narrow")
    rows, cols = w_hbm.shape
    steps = rows // ROWS
    blocks = ROWS // side
    tokens = nw * act_hbm.shape[0]

    def fetch(c):
        at = pl.ds(pl.multiple_of(c * ROWS, ROWS), ROWS)
        return pltpu.make_async_copy(w_hbm.at[at], w.at[at], w_sem.at[c])

    barrier = pltpu.get_barrier_semaphore()
    for off in range(1, nw):
        pl.semaphore_signal(
            barrier, inc=1, device_id={"wide": lax.rem(iw + off, nw)}, device_id_type=MESH
        )
    for off in range(1, nn):
        pl.semaphore_signal(
            barrier, inc=1, device_id={"narrow": lax.rem(jn + off, nn)}, device_id_type=MESH
        )
    own_copies = [
        pltpu.make_async_copy(mask_hbm, mask, in_sem.at[0]),
        pltpu.make_async_copy(act_hbm, act_all.at[iw], in_sem.at[1]),
        pltpu.make_async_copy(og_hbm, og_all.at[jn], in_sem.at[2]),
    ]
    for copy in own_copies:
        copy.start()
    for c in range(steps):
        fetch(c).start()

    at_col = lax.broadcasted_iota(jnp.int32, (cols // side, cols), 1)
    low = lax.broadcasted_iota(jnp.int32, (cols // side, cols), 0) * side
    spread = jnp.where((at_col >= low) & (at_col < low + side), 1.0, 0.0).astype(BF16)
    own_copies[0].wait()
    mask_out[...] = jnp.dot(
        mask[...].astype(F32).astype(BF16), spread, preferred_element_type=F32
    )

    pl.semaphore_wait(barrier, nw + nn - 2)

    def wide_copy(src, dst, send, recv, off):
        return pltpu.make_async_remote_copy(
            src_ref=src, dst_ref=dst, send_sem=send, recv_sem=recv,
            device_id={"wide": lax.rem(iw + off, nw)}, device_id_type=MESH,
        )

    def narrow_copy(src, dst, send, recv, to):
        return pltpu.make_async_remote_copy(
            src_ref=src, dst_ref=dst, send_sem=send, recv_sem=recv,
            device_id={"narrow": to}, device_id_type=MESH,
        )

    pair, place = jn // 2, jn % 2
    mate = pair * 2 + (1 - place)
    across = [lax.rem(pair + off, nn // 2) * 2 + place for off in range(nn // 2)]
    origin = [lax.rem(pair + nn // 2 - off, nn // 2) * 2 + place for off in range(nn // 2)]
    far = [
        narrow_copy(og_hbm, og_all.at[jn], og_send.at[off], og_recv.at[off], across[off])
        for off in range(1, nn // 2)
    ]
    near = [
        narrow_copy(
            og_hbm if off == 0 else og_all.at[origin[off]], og_all.at[origin[off]],
            og_send.at[nn // 2 + off], og_recv.at[nn // 2 + off], mate,
        )
        for off in range(nn // 2)
    ]
    act_copies = [
        wide_copy(act_hbm, act_all.at[iw], act_send.at[off], act_recv.at[off], off)
        for off in range(1, nw)
    ]
    for copy in far + near[:1] + act_copies:
        copy.start()

    def mask_rows(c):
        fetch(c).wait()
        for b in range(blocks):
            kept = mask_out[pl.ds(c * blocks + b, 1), :].astype(BF16)
            at = pl.ds(pl.multiple_of(c * ROWS + b * side, side), side)
            w[at, :] = w[at, :] * kept

    pl.loop(0, steps // 2)(mask_rows)
    for arrived, passed in zip(far, near[1:]):
        arrived.wait_recv()
        passed.start()
    pl.loop(steps // 2, steps)(mask_rows)

    for copy in far:
        copy.wait_send()
    for copy in near:
        copy.wait()
    for copy in own_copies[1:]:
        copy.wait()
    og_out[...] = og_all[...].reshape(tokens, cols)

    ig_copies = []
    for part, (start, stop) in enumerate(halves(steps)):

        @pl.loop(start, stop)
        def _(c):
            at = pl.ds(pl.multiple_of(c * ROWS, ROWS), ROWS)
            term = lax.dot_general(
                og_out[...], w[at, :], (((1,), (1,)), ((), ())), preferred_element_type=F32
            )
            ig_part[:, :, at] = term.reshape(nw, tokens // nw, ROWS).astype(BF16)

        at = pl.ds(start * ROWS, (stop - start) * ROWS)
        for off in range(1, nw):
            copy = wide_copy(
                ig_part.at[lax.rem(iw + off, nw), :, at], ig_recv.at[off, :, at],
                ig_send.at[part, off], ig_rsem.at[part, off], off,
            )
            copy.start()
            ig_copies.append(copy)

    for copy in act_copies:
        copy.wait()
    act_out[...] = act_all[...].astype(F32).reshape(tokens, rows).astype(BF16)

    wide_cols = column_chunk(cols)
    out_copies = []
    for part, (start, stop) in enumerate(halves(cols // wide_cols)):

        @pl.loop(start, stop)
        def _(c):
            at = pl.ds(pl.multiple_of(c * wide_cols, 128) if wide_cols < cols else 0, wide_cols)
            term = jnp.dot(act_out[...], w[:, at], preferred_element_type=F32)
            out_part[:, :, at] = term.astype(BF16).reshape(nn, tokens // nn, wide_cols)

        at = pl.ds(start * wide_cols, (stop - start) * wide_cols)
        for off in range(1, nn):
            to = lax.rem(jn + off, nn)
            copy = narrow_copy(
                out_part.at[to, :, at], out_recv.at[off, :, at],
                out_send.at[part, off], out_rsem.at[part, off], to,
            )
            copy.start()
            out_copies.append(copy)

    @pl.loop(0, grad_out.shape[0] // ROWS)
    def _(c):
        at = pl.multiple_of(c * ROWS, ROWS)
        grad_rows(side, act_out, og_out, mask_out, at, grad_out, at)

    for copy in ig_copies:
        copy.wait()
    total = ig_part[iw].astype(F32)
    for off in range(1, nw):
        total = total + ig_recv[off].astype(F32)
    ig_ref[...] = total.astype(BF16)

    for copy in out_copies:
        copy.wait()
    total = out_part[jn].astype(F32)
    for off in range(1, nn):
        total = total + out_recv[off].astype(F32)
    out_ref[...] = total.astype(BF16)


def weight_kernel(
    side, act_ref, og_ref, mask_ref, early_ref, out_in, ig_in,
    out_hbm, ig_hbm, grad_hbm, late, sems, late_sems,
):
    early = early_ref.shape[0]
    copies = [
        pltpu.make_async_copy(early_ref, grad_hbm.at[pl.ds(0, early)], sems.at[0]),
        pltpu.make_async_copy(out_in, out_hbm, sems.at[1]),
        pltpu.make_async_copy(ig_in, ig_hbm, sems.at[2]),
    ]
    for copy in copies:
        copy.start()

    def written(c):
        at = pl.multiple_of(c * ROWS, ROWS)
        return pltpu.make_async_copy(
            late.at[pl.ds(at, ROWS)], grad_hbm.at[pl.ds(early + at, ROWS)], late_sems.at[c]
        )

    count = late.shape[0] // ROWS

    @pl.loop(0, count)
    def _(c):
        at = pl.multiple_of(c * ROWS, ROWS)
        grad_rows(side, act_ref, og_ref, mask_ref, early + at, late, at)
        written(c).start()

    for copy in copies:
        copy.wait()
    for c in range(count):
        written(c).wait()


def on_device(nw, nn, activations, up_weight, block_mask, out_grad):
    rows, cols = up_weight.shape
    own_w, own_n = activations.shape[0], out_grad.shape[0]
    tokens = nw * own_w
    side = rows // block_mask.shape[0]
    early = rows // ROWS // 2 * ROWS
    vmem = pl.BlockSpec(memory_space=pltpu.VMEM)
    hbm = pl.BlockSpec(memory_space=pltpu.HBM)
    dma = pltpu.SemaphoreType.DMA
    shape = jax.ShapeDtypeStruct
    output, input_grad, act_all, og_all, mask_wide, grad_early = pl.pallas_call(
        functools.partial(exchange_kernel, nw, nn, side),
        out_shape=(
            shape((own_n, cols), BF16),
            shape((own_w, rows), BF16),
            shape((tokens, rows), BF16),
            shape((tokens, cols), BF16),
            shape((block_mask.shape[0], cols), F32),
            shape((early, cols), BF16),
        ),
        in_specs=[hbm] * 4,
        out_specs=(vmem,) * 6,
        scratch_shapes=[
            pltpu.VMEM((rows, cols), BF16),
            pltpu.VMEM(block_mask.shape, block_mask.dtype),
            pltpu.VMEM((nw, own_w, rows), BF16),
            pltpu.VMEM((nn, own_n, cols), BF16),
            pltpu.VMEM((nw, own_w, rows), BF16),
            pltpu.VMEM((nw, own_w, rows), BF16),
            pltpu.VMEM((nn, own_n, cols), BF16),
            pltpu.VMEM((nn, own_n, cols), BF16),
            dma((3,)),
            dma((rows // ROWS,)),
            dma((nw,)), dma((nw,)),
            dma((nn,)), dma((nn,)),
            dma((2, nw)), dma((2, nw)),
            dma((2, nn)), dma((2, nn)),
        ],
        compiler_params=pltpu.CompilerParams(
            collective_id=0, has_side_effects=True, vmem_limit_bytes=36 * 2**20
        ),
        cost_estimate=pl.CostEstimate(
            flops=4 * tokens * rows * cols, bytes_accessed=2 * rows * cols, transcendentals=0
        ),
        name="exchange",
    )(activations, up_weight, block_mask, out_grad)
    output, input_grad, weight_grad = pl.pallas_call(
        functools.partial(weight_kernel, side),
        out_shape=(
            shape((own_n, cols), BF16),
            shape((own_w, rows), BF16),
            shape((rows, cols), BF16),
        ),
        in_specs=[vmem] * 6,
        out_specs=(hbm,) * 3,
        scratch_shapes=[
            pltpu.VMEM((rows - early, cols), BF16),
            dma((3,)),
            dma(((rows - early) // ROWS,)),
        ],
        compiler_params=pltpu.CompilerParams(vmem_limit_bytes=28 * 2**20),
        cost_estimate=pl.CostEstimate(
            flops=2 * tokens * rows * cols, bytes_accessed=2 * rows * cols, transcendentals=0
        ),
        name="weight_grad",
    )(act_all, og_all, mask_wide, grad_early, output, input_grad)
    return (output, input_grad, weight_grad)


def solution(mesh):
    placed = (P("wide", "narrow"), P("narrow", "wide"), P("narrow", "wide"), P("narrow", "wide"))
    return jax.shard_map(
        functools.partial(on_device, mesh.shape["wide"], mesh.shape["narrow"]),
        mesh=mesh,
        in_specs=placed,
        out_specs=(P("narrow", "wide"), P("wide", "narrow"), P("narrow", "wide")),
        check_vma=False,
    )
```

```python
import functools

import jax
import jax.numpy as jnp
from jax import lax
from jax.experimental import pallas as pl
from jax.experimental.pallas import tpu as pltpu
from jax.sharding import PartitionSpec as P

MESH = pl.DeviceIdType.MESH
BF16 = jnp.bfloat16
F32 = jnp.float32
ROWS = 256


def column_chunk(cols):
    return 512 if cols % 512 == 0 else cols


def halves(count):
    middle = (count + 1) // 2
    return ((0, middle), (middle, count)) if count > 1 else ((0, count),)


def grad_rows(side, act_ref, og_ref, mask_ref, first, grad_ref, at):
    cols = og_ref.shape[1]
    tile_cols = 256 if cols % 256 == 0 else cols
    tile_rows = 2 * side
    turned = act_ref[:, pl.ds(first, ROWS)].T
    for r in range(ROWS // tile_rows):
        left = turned[r * tile_rows:(r + 1) * tile_rows]
        for c in range(cols // tile_cols):
            across = slice(c * tile_cols, (c + 1) * tile_cols)
            grad = jnp.dot(left, og_ref[:, across], preferred_element_type=F32).astype(BF16)
            for b in range(tile_rows // side):
                row = r * tile_rows + b * side
                kept = mask_ref[pl.ds((first + row) // side, 1), across].astype(BF16)
                grad_ref[pl.ds(at + row, side), across] = grad[b * side:(b + 1) * side] * kept


def exchange_kernel(
    nw, nn, side,
    act_hbm, w_hbm, mask_hbm, og_hbm,
    out_ref, ig_ref, act_out, og_out, mask_out, grad_out,
    w, mask, act_all, og_all, og_turned, ig_part, ig_recv, out_part, out_recv,
    in_sem, w_sem, act_send, act_recv, og_send, og_recv,
    ig_send, ig_rsem, out_send, out_rsem,
):
    iw = lax.axis_index("wide")
    jn = lax.axis_index("narrow")
    rows, cols = w_hbm.shape
    steps = rows // ROWS
    blocks = ROWS // side
    tokens = nw * act_hbm.shape[0]

    def fetch(c):
        at = pl.ds(pl.multiple_of(c * ROWS, ROWS), ROWS)
        return pltpu.make_async_copy(w_hbm.at[at], w.at[at], w_sem.at[c])

    barrier = pltpu.get_barrier_semaphore()
    for off in range(1, nw):
        pl.semaphore_signal(
            barrier, inc=1, device_id={"wide": lax.rem(iw + off, nw)}, device_id_type=MESH
        )
    for off in range(1, nn):
        pl.semaphore_signal(
            barrier, inc=1, device_id={"narrow": lax.rem(jn + off, nn)}, device_id_type=MESH
        )
    own_copies = [
        pltpu.make_async_copy(mask_hbm, mask, in_sem.at[0]),
        pltpu.make_async_copy(act_hbm, act_all.at[iw], in_sem.at[1]),
        pltpu.make_async_copy(og_hbm, og_all.at[jn], in_sem.at[2]),
    ]
    for copy in own_copies:
        copy.start()
    for c in range(steps):
        fetch(c).start()

    at_col = lax.broadcasted_iota(jnp.int32, (cols // side, cols), 1)
    low = lax.broadcasted_iota(jnp.int32, (cols // side, cols), 0) * side
    spread = jnp.where((at_col >= low) & (at_col < low + side), 1.0, 0.0).astype(BF16)
    own_copies[0].wait()
    mask_out[...] = jnp.dot(
        mask[...].astype(F32).astype(BF16), spread, preferred_element_type=F32
    )

    pl.semaphore_wait(barrier, nw + nn - 2)

    def wide_copy(src, dst, send, recv, off):
        return pltpu.make_async_remote_copy(
            src_ref=src, dst_ref=dst, send_sem=send, recv_sem=recv,
            device_id={"wide": lax.rem(iw + off, nw)}, device_id_type=MESH,
        )

    def narrow_copy(src, dst, send, recv, to):
        return pltpu.make_async_remote_copy(
            src_ref=src, dst_ref=dst, send_sem=send, recv_sem=recv,
            device_id={"narrow": to}, device_id_type=MESH,
        )

    pair, place = jn // 2, jn % 2
    mate = pair * 2 + (1 - place)
    across = [lax.rem(pair + off, nn // 2) * 2 + place for off in range(nn // 2)]
    origin = [lax.rem(pair + nn // 2 - off, nn // 2) * 2 + place for off in range(nn // 2)]
    far = [
        narrow_copy(og_hbm, og_all.at[jn], og_send.at[off], og_recv.at[off], across[off])
        for off in range(1, nn // 2)
    ]
    near = [
        narrow_copy(
            og_hbm if off == 0 else og_all.at[origin[off]], og_all.at[origin[off]],
            og_send.at[nn // 2 + off], og_recv.at[nn // 2 + off], mate,
        )
        for off in range(nn // 2)
    ]
    act_copies = [
        wide_copy(act_hbm, act_all.at[iw], act_send.at[off], act_recv.at[off], off)
        for off in range(1, nw)
    ]
    for copy in far + near[:1] + act_copies:
        copy.start()

    def mask_rows(c):
        fetch(c).wait()
        for b in range(blocks):
            kept = mask_out[pl.ds(c * blocks + b, 1), :].astype(BF16)
            at = pl.ds(pl.multiple_of(c * ROWS + b * side, side), side)
            w[at, :] = w[at, :] * kept

    ahead = steps - steps // 4
    pl.loop(0, ahead)(mask_rows)
    for arrived, passed in zip(far, near[1:]):
        arrived.wait_recv()
        passed.start()
    pl.loop(ahead, steps)(mask_rows)

    for copy in far:
        copy.wait_send()
    for copy in near:
        copy.wait()
    for copy in own_copies[1:]:
        copy.wait()
    og_out[...] = og_all[...].reshape(tokens, cols)
    og_turned[...] = og_out[...].T

    ig_copies = []
    for part, (start, stop) in enumerate(halves(steps)):

        @pl.loop(start, stop)
        def _(c):
            at = pl.ds(pl.multiple_of(c * ROWS, ROWS), ROWS)
            term = jnp.dot(w[at, :], og_turned[...], preferred_element_type=F32).T
            ig_part[:, :, at] = term.reshape(nw, tokens // nw, ROWS).astype(BF16)

        at = pl.ds(start * ROWS, (stop - start) * ROWS)
        for off in range(1, nw):
            copy = wide_copy(
                ig_part.at[lax.rem(iw + off, nw), :, at], ig_recv.at[off, :, at],
                ig_send.at[part, off], ig_rsem.at[part, off], off,
            )
            copy.start()
            ig_copies.append(copy)

    for copy in act_copies:
        copy.wait()
    act_out[...] = act_all[...].astype(F32).reshape(tokens, rows).astype(BF16)

    wide_cols = column_chunk(cols)
    out_copies = []
    for part, (start, stop) in enumerate(halves(cols // wide_cols)):

        @pl.loop(start, stop)
        def _(c):
            at = pl.ds(pl.multiple_of(c * wide_cols, 128) if wide_cols < cols else 0, wide_cols)
            term = jnp.dot(act_out[...], w[:, at], preferred_element_type=F32)
            out_part[:, :, at] = term.astype(BF16).reshape(nn, tokens // nn, wide_cols)

        at = pl.ds(start * wide_cols, (stop - start) * wide_cols)
        for off in range(1, nn):
            to = lax.rem(jn + off, nn)
            copy = narrow_copy(
                out_part.at[to, :, at], out_recv.at[off, :, at],
                out_send.at[part, off], out_rsem.at[part, off], to,
            )
            copy.start()
            out_copies.append(copy)

    @pl.loop(0, grad_out.shape[0] // ROWS)
    def _(c):
        at = pl.multiple_of(c * ROWS, ROWS)
        grad_rows(side, act_out, og_out, mask_out, at, grad_out, at)

    for copy in ig_copies:
        copy.wait()
    total = ig_part[iw].astype(F32)
    for off in range(1, nw):
        total = total + ig_recv[off].astype(F32)
    ig_ref[...] = total.astype(BF16)

    for copy in out_copies:
        copy.wait()
    total = out_part[jn].astype(F32)
    for off in range(1, nn):
        total = total + out_recv[off].astype(F32)
    out_ref[...] = total.astype(BF16)


def weight_kernel(
    side, act_ref, og_ref, mask_ref, early_ref, out_in, ig_in,
    out_hbm, ig_hbm, grad_hbm, late, sems, late_sems,
):
    early = early_ref.shape[0]
    copies = [
        pltpu.make_async_copy(early_ref, grad_hbm.at[pl.ds(0, early)], sems.at[0]),
        pltpu.make_async_copy(out_in, out_hbm, sems.at[1]),
        pltpu.make_async_copy(ig_in, ig_hbm, sems.at[2]),
    ]
    for copy in copies:
        copy.start()

    def written(c):
        at = pl.multiple_of(c * ROWS, ROWS)
        return pltpu.make_async_copy(
            late.at[pl.ds(at, ROWS)], grad_hbm.at[pl.ds(early + at, ROWS)], late_sems.at[c]
        )

    count = late.shape[0] // ROWS

    @pl.loop(0, count)
    def _(c):
        at = pl.multiple_of(c * ROWS, ROWS)
        grad_rows(side, act_ref, og_ref, mask_ref, early + at, late, at)
        written(c).start()

    for copy in copies:
        copy.wait()
    for c in range(count):
        written(c).wait()


def on_device(nw, nn, activations, up_weight, block_mask, out_grad):
    rows, cols = up_weight.shape
    own_w, own_n = activations.shape[0], out_grad.shape[0]
    tokens = nw * own_w
    side = rows // block_mask.shape[0]
    early = rows // ROWS // 2 * ROWS
    vmem = pl.BlockSpec(memory_space=pltpu.VMEM)
    hbm = pl.BlockSpec(memory_space=pltpu.HBM)
    dma = pltpu.SemaphoreType.DMA
    shape = jax.ShapeDtypeStruct
    output, input_grad, act_all, og_all, mask_wide, grad_early = pl.pallas_call(
        functools.partial(exchange_kernel, nw, nn, side),
        out_shape=(
            shape((own_n, cols), BF16),
            shape((own_w, rows), BF16),
            shape((tokens, rows), BF16),
            shape((tokens, cols), BF16),
            shape((block_mask.shape[0], cols), F32),
            shape((early, cols), BF16),
        ),
        in_specs=[hbm] * 4,
        out_specs=(vmem,) * 6,
        scratch_shapes=[
            pltpu.VMEM((rows, cols), BF16),
            pltpu.VMEM(block_mask.shape, block_mask.dtype),
            pltpu.VMEM((nw, own_w, rows), BF16),
            pltpu.VMEM((nn, own_n, cols), BF16),
            pltpu.VMEM((cols, tokens), BF16),
            pltpu.VMEM((nw, own_w, rows), BF16),
            pltpu.VMEM((nw, own_w, rows), BF16),
            pltpu.VMEM((nn, own_n, cols), BF16),
            pltpu.VMEM((nn, own_n, cols), BF16),
            dma((3,)),
            dma((rows // ROWS,)),
            dma((nw,)), dma((nw,)),
            dma((nn,)), dma((nn,)),
            dma((2, nw)), dma((2, nw)),
            dma((2, nn)), dma((2, nn)),
        ],
        compiler_params=pltpu.CompilerParams(
            collective_id=0, has_side_effects=True, vmem_limit_bytes=36 * 2**20
        ),
        cost_estimate=pl.CostEstimate(
            flops=4 * tokens * rows * cols, bytes_accessed=2 * rows * cols, transcendentals=0
        ),
        name="exchange",
    )(activations, up_weight, block_mask, out_grad)
    output, input_grad, weight_grad = pl.pallas_call(
        functools.partial(weight_kernel, side),
        out_shape=(
            shape((own_n, cols), BF16),
            shape((own_w, rows), BF16),
            shape((rows, cols), BF16),
        ),
        in_specs=[vmem] * 6,
        out_specs=(hbm,) * 3,
        scratch_shapes=[
            pltpu.VMEM((rows - early, cols), BF16),
            dma((3,)),
            dma(((rows - early) // ROWS,)),
        ],
        compiler_params=pltpu.CompilerParams(vmem_limit_bytes=28 * 2**20),
        cost_estimate=pl.CostEstimate(
            flops=2 * tokens * rows * cols, bytes_accessed=2 * rows * cols, transcendentals=0
        ),
        name="weight_grad",
    )(act_all, og_all, mask_wide, grad_early, output, input_grad)
    return (output, input_grad, weight_grad)


def solution(mesh):
    placed = (P("wide", "narrow"), P("narrow", "wide"), P("narrow", "wide"), P("narrow", "wide"))
    return jax.shard_map(
        functools.partial(on_device, mesh.shape["wide"], mesh.shape["narrow"]),
        mesh=mesh,
        in_specs=placed,
        out_specs=(P("narrow", "wide"), P("wide", "narrow"), P("narrow", "wide")),
        check_vma=False,
    )
```

```python
import functools

import jax
import jax.numpy as jnp
from jax import lax
from jax.experimental import pallas as pl
from jax.experimental.pallas import tpu as pltpu
from jax.sharding import PartitionSpec as P

MESH = pl.DeviceIdType.MESH
BF16 = jnp.bfloat16
F32 = jnp.float32
ROWS = 256


def column_chunk(cols):
    return 512 if cols % 512 == 0 else cols


def halves(count):
    middle = (count + 1) // 2
    return ((0, middle), (middle, count)) if count > 1 else ((0, count),)


def grad_rows(side, act_ref, og_ref, mask_ref, first, grad_ref, at):
    cols = og_ref.shape[1]
    tile_cols = 256 if cols % 256 == 0 else cols
    tile_rows = ROWS
    turned = act_ref[:, pl.ds(first, ROWS)].T
    for r in range(ROWS // tile_rows):
        left = turned[r * tile_rows:(r + 1) * tile_rows]
        for c in range(cols // tile_cols):
            across = slice(c * tile_cols, (c + 1) * tile_cols)
            grad = jnp.dot(left, og_ref[:, across], preferred_element_type=F32).astype(BF16)
            for b in range(tile_rows // side):
                row = r * tile_rows + b * side
                kept = mask_ref[pl.ds((first + row) // side, 1), across].astype(BF16)
                grad_ref[pl.ds(at + row, side), across] = grad[b * side:(b + 1) * side] * kept


def exchange_kernel(
    nw, nn, side,
    act_hbm, w_hbm, mask_hbm, og_hbm,
    out_ref, ig_ref, act_out, og_out, mask_out, grad_out,
    w, mask, act_all, og_all, ig_part, ig_recv, out_part, out_recv,
    in_sem, w_sem, act_send, act_recv, og_send, og_recv,
    ig_send, ig_rsem, out_send, out_rsem,
):
    iw = lax.axis_index("wide")
    jn = lax.axis_index("narrow")
    rows, cols = w_hbm.shape
    steps = rows // ROWS
    blocks = ROWS // side
    tokens = nw * act_hbm.shape[0]

    def fetch(c):
        at = pl.ds(pl.multiple_of(c * ROWS, ROWS), ROWS)
        return pltpu.make_async_copy(w_hbm.at[at], w.at[at], w_sem.at[c])

    barrier = pltpu.get_barrier_semaphore()
    for off in range(1, nw):
        pl.semaphore_signal(
            barrier, inc=1, device_id={"wide": lax.rem(iw + off, nw)}, device_id_type=MESH
        )
    for off in range(1, nn):
        pl.semaphore_signal(
            barrier, inc=1, device_id={"narrow": lax.rem(jn + off, nn)}, device_id_type=MESH
        )
    own_copies = [
        pltpu.make_async_copy(mask_hbm, mask, in_sem.at[0]),
        pltpu.make_async_copy(act_hbm, act_all.at[iw], in_sem.at[1]),
        pltpu.make_async_copy(og_hbm, og_all.at[jn], in_sem.at[2]),
    ]
    for copy in own_copies:
        copy.start()
    for c in range(steps):
        fetch(c).start()

    at_col = lax.broadcasted_iota(jnp.int32, (cols // side, cols), 1)
    low = lax.broadcasted_iota(jnp.int32, (cols // side, cols), 0) * side
    spread = jnp.where((at_col >= low) & (at_col < low + side), 1.0, 0.0).astype(BF16)
    own_copies[0].wait()
    mask_out[...] = jnp.dot(
        mask[...].astype(F32).astype(BF16), spread, preferred_element_type=F32
    )

    pl.semaphore_wait(barrier, nw + nn - 2)

    def wide_copy(src, dst, send, recv, off):
        return pltpu.make_async_remote_copy(
            src_ref=src, dst_ref=dst, send_sem=send, recv_sem=recv,
            device_id={"wide": lax.rem(iw + off, nw)}, device_id_type=MESH,
        )

    def narrow_copy(src, dst, send, recv, to):
        return pltpu.make_async_remote_copy(
            src_ref=src, dst_ref=dst, send_sem=send, recv_sem=recv,
            device_id={"narrow": to}, device_id_type=MESH,
        )

    pair, place = jn // 2, jn % 2
    mate = pair * 2 + (1 - place)
    across = [lax.rem(pair + off, nn // 2) * 2 + place for off in range(nn // 2)]
    origin = [lax.rem(pair + nn // 2 - off, nn // 2) * 2 + place for off in range(nn // 2)]
    far = [
        narrow_copy(og_hbm, og_all.at[jn], og_send.at[off], og_recv.at[off], across[off])
        for off in range(1, nn // 2)
    ]
    near = [
        narrow_copy(
            og_hbm if off == 0 else og_all.at[origin[off]], og_all.at[origin[off]],
            og_send.at[nn // 2 + off], og_recv.at[nn // 2 + off], mate,
        )
        for off in range(nn // 2)
    ]
    act_copies = [
        wide_copy(act_hbm, act_all.at[iw], act_send.at[off], act_recv.at[off], off)
        for off in range(1, nw)
    ]
    for copy in far + near[:1] + act_copies:
        copy.start()

    def mask_rows(c):
        fetch(c).wait()
        for b in range(blocks):
            kept = mask_out[pl.ds(c * blocks + b, 1), :].astype(BF16)
            at = pl.ds(pl.multiple_of(c * ROWS + b * side, side), side)
            w[at, :] = w[at, :] * kept

    pl.loop(0, steps // 2)(mask_rows)
    for arrived, passed in zip(far, near[1:]):
        arrived.wait_recv()
        passed.start()
    pl.loop(steps // 2, steps)(mask_rows)

    for copy in far:
        copy.wait_send()
    for copy in near:
        copy.wait()
    for copy in own_copies[1:]:
        copy.wait()
    og_out[...] = og_all[...].reshape(tokens, cols)

    ig_copies = []
    for part, (start, stop) in enumerate(halves(steps)):

        @pl.loop(start, stop)
        def _(c):
            at = pl.ds(pl.multiple_of(c * ROWS, ROWS), ROWS)
            term = lax.dot_general(
                og_out[...], w[at, :], (((1,), (1,)), ((), ())), preferred_element_type=F32
            )
            ig_part[:, :, at] = term.reshape(nw, tokens // nw, ROWS).astype(BF16)

        at = pl.ds(start * ROWS, (stop - start) * ROWS)
        for off in range(1, nw):
            copy = wide_copy(
                ig_part.at[lax.rem(iw + off, nw), :, at], ig_recv.at[off, :, at],
                ig_send.at[part, off], ig_rsem.at[part, off], off,
            )
            copy.start()
            ig_copies.append(copy)

    for copy in act_copies:
        copy.wait()
    act_out[...] = act_all[...].astype(F32).reshape(tokens, rows).astype(BF16)

    wide_cols = column_chunk(cols)
    out_copies = []
    for part, (start, stop) in enumerate(halves(cols // wide_cols)):

        @pl.loop(start, stop)
        def _(c):
            at = pl.ds(pl.multiple_of(c * wide_cols, 128) if wide_cols < cols else 0, wide_cols)
            term = jnp.dot(act_out[...], w[:, at], preferred_element_type=F32)
            out_part[:, :, at] = term.astype(BF16).reshape(nn, tokens // nn, wide_cols)

        at = pl.ds(start * wide_cols, (stop - start) * wide_cols)
        for off in range(1, nn):
            to = lax.rem(jn + off, nn)
            copy = narrow_copy(
                out_part.at[to, :, at], out_recv.at[off, :, at],
                out_send.at[part, off], out_rsem.at[part, off], to,
            )
            copy.start()
            out_copies.append(copy)

    @pl.loop(0, grad_out.shape[0] // ROWS)
    def _(c):
        at = pl.multiple_of(c * ROWS, ROWS)
        grad_rows(side, act_out, og_out, mask_out, at, grad_out, at)

    for copy in ig_copies:
        copy.wait()
    total = ig_part[iw].astype(F32)
    for off in range(1, nw):
        total = total + ig_recv[off].astype(F32)
    ig_ref[...] = total.astype(BF16)

    for copy in out_copies:
        copy.wait()
    total = out_part[jn].astype(F32)
    for off in range(1, nn):
        total = total + out_recv[off].astype(F32)
    out_ref[...] = total.astype(BF16)


def weight_kernel(
    side, act_ref, og_ref, mask_ref, early_ref, out_in, ig_in,
    out_hbm, ig_hbm, grad_hbm, late, sems, late_sems,
):
    early = early_ref.shape[0]
    copies = [
        pltpu.make_async_copy(early_ref, grad_hbm.at[pl.ds(0, early)], sems.at[0]),
        pltpu.make_async_copy(out_in, out_hbm, sems.at[1]),
        pltpu.make_async_copy(ig_in, ig_hbm, sems.at[2]),
    ]
    for copy in copies:
        copy.start()

    def written(c):
        at = pl.multiple_of(c * ROWS, ROWS)
        return pltpu.make_async_copy(
            late.at[pl.ds(at, ROWS)], grad_hbm.at[pl.ds(early + at, ROWS)], late_sems.at[c]
        )

    count = late.shape[0] // ROWS

    @pl.loop(0, count)
    def _(c):
        at = pl.multiple_of(c * ROWS, ROWS)
        grad_rows(side, act_ref, og_ref, mask_ref, early + at, late, at)
        written(c).start()

    for copy in copies:
        copy.wait()
    for c in range(count):
        written(c).wait()


def on_device(nw, nn, activations, up_weight, block_mask, out_grad):
    rows, cols = up_weight.shape
    own_w, own_n = activations.shape[0], out_grad.shape[0]
    tokens = nw * own_w
    side = rows // block_mask.shape[0]
    early = rows // ROWS // 2 * ROWS
    vmem = pl.BlockSpec(memory_space=pltpu.VMEM)
    hbm = pl.BlockSpec(memory_space=pltpu.HBM)
    dma = pltpu.SemaphoreType.DMA
    shape = jax.ShapeDtypeStruct
    output, input_grad, act_all, og_all, mask_wide, grad_early = pl.pallas_call(
        functools.partial(exchange_kernel, nw, nn, side),
        out_shape=(
            shape((own_n, cols), BF16),
            shape((own_w, rows), BF16),
            shape((tokens, rows), BF16),
            shape((tokens, cols), BF16),
            shape((block_mask.shape[0], cols), F32),
            shape((early, cols), BF16),
        ),
        in_specs=[hbm] * 4,
        out_specs=(vmem,) * 6,
        scratch_shapes=[
            pltpu.VMEM((rows, cols), BF16),
            pltpu.VMEM(block_mask.shape, block_mask.dtype),
            pltpu.VMEM((nw, own_w, rows), BF16),
            pltpu.VMEM((nn, own_n, cols), BF16),
            pltpu.VMEM((nw, own_w, rows), BF16),
            pltpu.VMEM((nw, own_w, rows), BF16),
            pltpu.VMEM((nn, own_n, cols), BF16),
            pltpu.VMEM((nn, own_n, cols), BF16),
            dma((3,)),
            dma((rows // ROWS,)),
            dma((nw,)), dma((nw,)),
            dma((nn,)), dma((nn,)),
            dma((2, nw)), dma((2, nw)),
            dma((2, nn)), dma((2, nn)),
        ],
        compiler_params=pltpu.CompilerParams(
            collective_id=0, has_side_effects=True, vmem_limit_bytes=36 * 2**20
        ),
        cost_estimate=pl.CostEstimate(
            flops=4 * tokens * rows * cols, bytes_accessed=2 * rows * cols, transcendentals=0
        ),
        name="exchange",
    )(activations, up_weight, block_mask, out_grad)
    output, input_grad, weight_grad = pl.pallas_call(
        functools.partial(weight_kernel, side),
        out_shape=(
            shape((own_n, cols), BF16),
            shape((own_w, rows), BF16),
            shape((rows, cols), BF16),
        ),
        in_specs=[vmem] * 6,
        out_specs=(hbm,) * 3,
        scratch_shapes=[
            pltpu.VMEM((rows - early, cols), BF16),
            dma((3,)),
            dma(((rows - early) // ROWS,)),
        ],
        compiler_params=pltpu.CompilerParams(vmem_limit_bytes=28 * 2**20),
        cost_estimate=pl.CostEstimate(
            flops=2 * tokens * rows * cols, bytes_accessed=2 * rows * cols, transcendentals=0
        ),
        name="weight_grad",
    )(act_all, og_all, mask_wide, grad_early, output, input_grad)
    return (output, input_grad, weight_grad)


def solution(mesh):
    placed = (P("wide", "narrow"), P("narrow", "wide"), P("narrow", "wide"), P("narrow", "wide"))
    return jax.shard_map(
        functools.partial(on_device, mesh.shape["wide"], mesh.shape["narrow"]),
        mesh=mesh,
        in_specs=placed,
        out_specs=(P("narrow", "wide"), P("wide", "narrow"), P("narrow", "wide")),
        check_vma=False,
    )
```
